512 devices in a mesh: dp: 32 (over x_hi, z, core), mp: 16 (over x_lo, y).
Axes of the slice: x: 4 (x_hi: 2, x_lo: 2; x = x_hi * 2 + x_lo), y: 8, z: 8, core: 2. Of those that a mesh axis runs over, the one named last changes fastest.
Arguments:
- activations: bfloat16 [16384, 3072], P('dp'), may hold values from -48 to 48
- output_grad: bfloat16 [16384, 12288], P('dp', 'mp'), may hold values from -48 to 48
- weight_grad: bfloat16 [3072, 12288], P('dp', 'mp'), may hold values from -4 to 4
- input_basis: bfloat16 [3072, 3072], P(None, 'dp'), may hold values from -0.109375 to 0.109375
- input_eigen: float32 [3072], P('dp'), may hold values from 0.1 to 3
- output_basis: bfloat16 [16, 768, 768], P('mp', 'dp'), may hold values from -0.21875 to 0.21875
- output_eigen: float32 [16, 768], P('mp'), may hold values from 0.1 to 3
- input_factor: float32 [3072, 3072], P('mp', 'dp'), may hold values from -0.06 to 5
- output_factor: float32 [16, 768, 768], P('mp', 'dp'), may hold values from -0.06 to 5
Outputs:
- new_input_factor: float32 [3072, 3072], P('mp', 'dp')
- new_output_factor: float32 [16, 768, 768], P('mp', 'dp')
- preconditioned: bfloat16 [3072, 12288], P('dp', 'mp')
The draws below stay inside these ranges and needn't reach their ends.
All inputs are finite; a program needn't handle non-finite values.
Results may differ from the reference program's by a relative error of at most 0.025.
Values may be sent and summed in bfloat16 or wider, within the bound.
No kernel may reach another device: no remote copies, remote signals or barrier semaphores. Data moves between devices by JAX's collectives and lax.ppermute only.
A program may use at most 64 MiB of HBM per device.

```python
import math
import jax
import jax.numpy as jnp
from jax import lax

D = 3072
HS = 768
TOK_DP = 512
TOKENS = 16384
H = 12288
N_DP = 32
N_MP = 16


def group_rise(row_count, group_rows):
    group_total = max(row_count // group_rows, 2)
    group_ids = (lax.broadcasted_iota(jnp.int32, (row_count, 1), 0) // group_rows).astype(jnp.float32)
    return jnp.exp(1.5 * group_ids / (group_total - 1))


def shaped_rows(key, noise_part, strength, row_spread, col_spread, group_rows):
    row_count, col_count = noise_part.shape
    key_row, key_col, key_common, key_direction = jax.random.split(key, 4)
    row_scale = jnp.exp(jax.random.uniform(key_row, (row_count, 1), jnp.float32, -0.5, 0.5) * math.log(row_spread))
    row_scale = row_scale * group_rise(row_count, group_rows)
    col_scale = jnp.exp(jax.random.uniform(key_col, (1, col_count), jnp.float32, -0.5, 0.5) * math.log(col_spread))
    common = jnp.clip(jax.random.normal(key_common, (row_count, 1), jnp.float32), -4.0, 4.0)
    direction = jnp.clip(jax.random.normal(key_direction, (1, col_count), jnp.float32), -4.0, 4.0)
    values = row_scale * col_scale * (noise_part + strength * common * direction)
    return jnp.clip(values, -48.0, 48.0)


def running_factor(key, count, leading, lowest, highest, spread):
    key_diag, key_off = jax.random.split(key)
    diag_values = jnp.exp(jax.random.uniform(key_diag, leading + (1, count), jnp.float32, math.log(lowest), math.log(highest)))
    off_part = jnp.clip(jax.random.normal(key_off, leading + (count, count), jnp.float32), -4.0, 4.0)
    symmetric = (off_part + jnp.swapaxes(off_part, -1, -2)) * (0.7071 * spread)
    row_ids = lax.broadcasted_iota(jnp.int32, (count, count), 0)
    col_ids = lax.broadcasted_iota(jnp.int32, (count, count), 1)
    return jnp.where(row_ids == col_ids, diag_values, symmetric)


def draw_activations(key, part):
    key = jax.random.fold_in(key, 11)
    key_noise, key_shape = jax.random.split(key)
    noise_part = jnp.clip(jax.random.normal(key_noise, (TOKENS, D), jnp.float32), -4.0, 4.0)
    values = shaped_rows(key_shape, noise_part, 0.3, 4.0, 6.25, TOK_DP)
    return values.astype(jnp.bfloat16)


def draw_output_grad(key, part):
    key = jax.random.fold_in(key, 17)
    key_noise, key_shape = jax.random.split(key)
    noise_part = jnp.clip(jax.random.normal(key_noise, (TOKENS, H), jnp.float32), -4.0, 4.0)
    values = shaped_rows(key_shape, noise_part, 0.3, 4.0, 6.25, TOK_DP)
    return values.astype(jnp.bfloat16)


def draw_input_factor(key, part):
    key = jax.random.fold_in(key, 23)
    values = running_factor(key, D, (), 0.3, 3.0, 0.01)
    return values.astype(jnp.float32)


def draw_output_factor(key, part):
    key = jax.random.fold_in(key, 29)
    values = running_factor(key, HS, (N_MP,), 0.3, 3.0, 0.01)
    return values.astype(jnp.float32)


def levels(key, extent, pieces, least, top_value):
    level, own = 1.0, jax.random.fold_in(key, 6)
    for axis_at, blocks in pieces:
        steps = jnp.exp(jax.random.uniform(jax.random.fold_in(own, axis_at), (blocks,), jnp.float32, least / len(pieces), top_value / len(pieces)))
        level = level * jnp.repeat(steps, extent[axis_at] // blocks).reshape([-1 if axis == axis_at else 1 for axis in range(len(extent))])
    return level


def scatter_about(stream_key, extent, scale, limit, cuts=(), held_as=jnp.bfloat16):
    result = jax.random.normal(stream_key, extent, jnp.float32) * scale
    if len(cuts) > 0:
        result = levels(stream_key, extent, cuts, -0.22, 0.18) * result
    return jnp.clip(result, min=-limit, max=limit).astype(held_as)


def setup_inputs(seed: int = 0) -> dict:
    key_list = jax.random.split(jax.random.key(seed), 10)
    activations = draw_activations(jax.random.fold_in(key_list[9], 71), 0)
    output_grad = draw_output_grad(jax.random.fold_in(key_list[9], 71), 0)
    weight_grad = scatter_about(key_list[2], (D, H), 0.3, 4.0, ((0, 32), (1, 16)))
    input_basis = scatter_about(key_list[3], (D, D), D ** -0.5, 0.109375, ((1, 32),))
    input_eigen = jnp.clip(jnp.exp(math.log(3.0) - 3.4011974 * jax.random.uniform(key_list[4], (D,), jnp.float32) ** levels(key_list[4], (D,), ((0, 32),), -0.2, 0.2)), 0.1, 3.0)
    output_basis = scatter_about(key_list[5], (N_MP, HS, HS), HS ** -0.5, 0.21875, ((0, 16), (1, 32)))
    output_eigen = jnp.clip(jnp.exp(math.log(3.0) - 3.4011974 * jax.random.uniform(key_list[6], (N_MP, HS), jnp.float32) ** levels(key_list[6], (N_MP, HS), ((0, 16),), -0.2, 0.2)), 0.1, 3.0)
    input_factor = draw_input_factor(jax.random.fold_in(key_list[9], 71), 0)
    output_factor = draw_output_factor(jax.random.fold_in(key_list[9], 71), 0)
    return dict(activations=activations, output_grad=output_grad, weight_grad=weight_grad, input_basis=input_basis, input_eigen=input_eigen, output_basis=output_basis, output_eigen=output_eigen, input_factor=input_factor, output_factor=output_factor)


keep_rate = 0.95
damping = 0.03


def reference(activations, output_grad, weight_grad, input_basis, input_eigen, output_basis, output_eigen, input_factor, output_factor):
    act_groups = activations.reshape(N_DP, TOK_DP, D)
    grad_groups = output_grad.reshape(N_DP, TOK_DP, N_MP, HS)

    def add_input(running, group_rows):
        partial_sum = jnp.dot(group_rows.T, group_rows, preferred_element_type=jnp.float32).astype(jnp.bfloat16)
        partial_sum = lax.optimization_barrier(partial_sum)
        return running + partial_sum.astype(jnp.float32), 0

    def add_output(running, group_rows):
        rows_wide = group_rows.astype(jnp.float32)
        partial_sum = jnp.einsum("tbi,tbj->bij", rows_wide, rows_wide).astype(jnp.bfloat16)
        partial_sum = lax.optimization_barrier(partial_sum)
        return running + partial_sum.astype(jnp.float32), 0

    input_sum, _ = lax.scan(add_input, jnp.zeros((D, D), jnp.float32), act_groups)
    output_sum, _ = lax.scan(add_output, jnp.zeros((N_MP, HS, HS), jnp.float32), grad_groups)
    new_input = keep_rate * input_factor + (1.0 - keep_rate) * (input_sum / TOKENS)
    new_output = keep_rate * output_factor + (1.0 - keep_rate) * (output_sum / TOKENS)

    blocks_out = []
    for shard in range(N_MP):
        grad_block = weight_grad[:, shard * HS:(shard + 1) * HS]
        left_part = jnp.dot(input_basis.T, grad_block, preferred_element_type=jnp.float32).astype(jnp.bfloat16)
        rotated = jnp.dot(left_part, output_basis[shard], preferred_element_type=jnp.float32)
        denominator = input_eigen[:, None] * output_eigen[shard][None, :] + damping
        scaled = (rotated / denominator).astype(jnp.bfloat16)
        back_part = jnp.dot(scaled, output_basis[shard].T, preferred_element_type=jnp.float32).astype(jnp.bfloat16)
        blocks_out.append(jnp.dot(input_basis, back_part, preferred_element_type=jnp.float32).astype(jnp.bfloat16))
    return new_input, new_output, jnp.concatenate(blocks_out, axis=1)
```

```python
import jax
import jax.numpy as jnp
from jax import lax
from jax.sharding import Mesh, PartitionSpec as P

keep_rate = 0.95
damping = 0.03
swap = ((0, 1), (1, 0))
DP = ("xh", "z", "c")
MP = ("xl", "y")


def dot(a, b, da, db):
    return lax.dot_general(a, b, (((da,), (db,)), ((), ())), preferred_element_type=jnp.float32)


def pick(a, index, axis):
    return lax.dynamic_index_in_dim(a, index, axis, keepdims=False)


def per_device(
    activations,
    output_grad,
    weight_grad,
    input_basis,
    input_eigen,
    output_basis,
    output_eigen,
    input_factor,
    output_factor,
):
    bf16, f32 = jnp.bfloat16, jnp.float32
    xh, c = lax.axis_index("xh"), lax.axis_index("c")
    m = lax.axis_index(MP)
    tokens = activations.shape[0] * 32

    halves = weight_grad.reshape(96, 2, 384).transpose(1, 0, 2)
    send = jnp.broadcast_to(halves[None], (8, 2, 96, 384)).reshape(16, 96, 384)
    grad_rows = lax.all_to_all(send, ("z", "c"), 0, 0).reshape(1536, 384)

    basis_out = output_basis[0]
    basis_far = lax.ppermute(basis_out, "xh", swap)
    basis_pair = jnp.where(xh == 0, jnp.stack([basis_out, basis_far]), jnp.stack([basis_far, basis_out]))
    basis_all = lax.all_gather(basis_pair, ("z", "c"), axis=0)
    v_rel = jnp.concatenate([pick(basis_all, c, 1), pick(basis_all, 1 - c, 1)], axis=0).reshape(768, 768)

    ut = input_basis.T
    ut_mine = lax.dynamic_slice_in_dim(ut, xh * 1536, 1536, 1)
    ut_other = lax.dynamic_slice_in_dim(ut, (1 - xh) * 1536, 1536, 1)
    ut_far = lax.ppermute(ut_other, "xh", swap)
    mine = jnp.stack([ut_mine, ut_far])
    theirs = lax.ppermute(mine, "c", swap)
    first = jnp.stack([mine, theirs], axis=1).reshape(384, 1536)

    selected = lax.dynamic_slice_in_dim(activations, m * 192, 192, 1)
    input_term = dot(activations, selected, 0, 0).astype(bf16)
    output_term = dot(output_grad, output_grad, 0, 0).astype(bf16)
    in_parts = input_term.reshape(2, 8, 2, 96, 192).transpose(2, 1, 3, 0, 4).reshape(2, 8, 96, 384)
    out_parts = output_term.reshape(2, 8, 2, 24, 2, 384).transpose(2, 1, 4, 0, 3, 5).reshape(2, 8, 96, 384)
    parts = jnp.concatenate([in_parts, out_parts], axis=2)
    came = lax.ppermute(pick(parts, 1 - c, 0), "c", swap)
    pair = (pick(parts, c, 0).astype(f32) + came.astype(f32)).astype(bf16)
    summed = lax.psum_scatter(pair, "z", scatter_dimension=0, tiled=False)
    in_sum = summed[:96].reshape(96, 2, 192)
    out_sum = summed[96:].reshape(2, 2, 24, 384)
    in_came = lax.ppermute(pick(in_sum, 1 - xh, 1), "xh", swap)
    out_came = lax.ppermute(pick(out_sum, 1 - xh, 1), "xh", swap)
    in_total = pick(in_sum, xh, 1).astype(f32) + in_came.astype(f32)
    out_total = pick(out_sum, xh, 1).astype(f32) + out_came.astype(f32)
    new_input = keep_rate * input_factor + (1.0 - keep_rate) * (in_total.T / tokens)
    new_output = keep_rate * output_factor + (1.0 - keep_rate) * (
        out_total.transpose(1, 0, 2).reshape(1, 24, 768) / tokens
    )

    left_part = dot(first, grad_rows, 1, 0).reshape(2, 2, 96, 384)
    left_came = lax.ppermute(left_part[1].astype(bf16), "xh", swap)
    left_two = (left_part[0] + left_came.astype(f32)).astype(bf16)
    left_far = lax.ppermute(left_two[1], "c", swap)
    left = jnp.concatenate([left_two[0], left_far], axis=1)
    rotated = dot(left, v_rel, 1, 0)
    denominator = input_eigen[:, None] * output_eigen[0][None, :] + damping
    scaled = (rotated / denominator).astype(bf16)
    back = dot(scaled, v_rel, 1, 1).astype(bf16)

    rel = jnp.stack([ut_mine, ut_other], axis=1).reshape(96, 2, 8, 192).transpose(2, 0, 1, 3).reshape(8, 96, 384)
    slab = lax.all_to_all(rel, "z", 0, 0)
    slab_far = lax.ppermute(slab, "c", swap)
    second = jnp.where(
        c == 0, jnp.stack([slab, slab_far], axis=1), jnp.stack([slab_far, slab], axis=1)
    ).reshape(1536, 384)

    near, far = back[:, :384], back[:, 384:]
    back_halves = jnp.where(c == 0, jnp.stack([near, far]), jnp.stack([far, near]))
    send = jnp.broadcast_to(back_halves[None], (8, 2, 96, 384)).reshape(16, 96, 384)
    back_rows = lax.all_to_all(send, ("z", "c"), 0, 0).reshape(1536, 384)
    out_part = dot(second, back_rows, 0, 0).reshape(2, 192, 384)
    out_far = lax.ppermute(out_part[1].astype(bf16), "xh", swap)
    out_two = (out_part[0] + out_far.astype(f32)).astype(bf16).reshape(2, 96, 384)
    result = lax.all_to_all(out_two, "c", 0, 0).transpose(1, 0, 2).reshape(96, 768)
    return (new_input, new_output, result)


def solution(mesh):
    fine = Mesh(mesh.devices.reshape(2, 8, 2, 2, 8), DP + MP)
    placed = (
        P(DP, None),
        P(DP, MP),
        P(DP, MP),
        P(None, DP),
        P(DP),
        P(MP, DP, None),
        P(MP, None),
        P(MP, DP),
        P(MP, DP, None),
    )
    return jax.shard_map(
        per_device,
        mesh=fine,
        in_specs=placed,
        out_specs=(P(MP, DP), P(MP, DP, None), P(DP, MP)),
        check_vma=False,
    )
```

```python
import jax
import jax.numpy as jnp
from jax import lax
from jax.experimental import pallas as pl
from jax.experimental.pallas import tpu as pltpu
from jax.sharding import Mesh, PartitionSpec as P

keep_rate = 0.95
damping = 0.03
swap = ((0, 1), (1, 0))
DP = ("xh", "z", "c")
MP = ("xl", "y")
QUAD = ("xh", "c")
bf16, f32 = jnp.bfloat16, jnp.float32


def dot(a, b, da, db):
    return lax.dot_general(a, b, (((da,), (db,)), ((), ())), preferred_element_type=f32)


def pick(a, index, axis):
    return lax.dynamic_index_in_dim(a, index, axis, keepdims=False)


def factor_kernel(core, act, sel, grad, mine, other, t_in, t_out):
    c = core[0]
    for j in range(4):
        low = act[:, j * 384 : (j + 1) * 384]
        high = act[:, 1536 + j * 384 : 1536 + (j + 1) * 384]
        t_in[j * 384 : (j + 1) * 384, :] = (dot(low, sel[0], 0, 0) + dot(high, sel[1], 0, 0)).astype(bf16)
    for j in range(2):
        t_out[j * 384 : (j + 1) * 384, :] = dot(grad[:, j * 384 : (j + 1) * 384], grad[...], 0, 0)
    for target, core_at in ((mine, c), (other, 1 - c)):
        for z in range(8):
            row = pl.multiple_of(z * 192 + core_at * 96, 96)
            target[z, 0:96, :] = t_in[pl.ds(row, 96), :]
            row = pl.multiple_of(z * 48 + core_at * 24, 24)
            first, second = t_out[pl.ds(row, 24), :], t_out[pl.ds(pl.multiple_of(384 + row, 24), 24), :]
            pair = jnp.concatenate([first, second], axis=0).astype(bf16)
            target[z, 96:144, :] = pair[:, :384]
            target[z, 144:192, :] = pair[:, 384:]


def factor_parts(core, act, sel, grad):
    vmem = pl.BlockSpec(memory_space=pltpu.VMEM)
    return pl.pallas_call(
        factor_kernel,
        out_shape=[jax.ShapeDtypeStruct((8, 192, 384), bf16)] * 2,
        in_specs=[pl.BlockSpec(memory_space=pltpu.SMEM), vmem, vmem, vmem],
        out_specs=[vmem, vmem],
        scratch_shapes=[pltpu.VMEM((1536, 384), bf16), pltpu.VMEM((768, 768), f32)],
        compiler_params=pltpu.CompilerParams(vmem_limit_bytes=32 * 1024 * 1024),
        cost_estimate=pl.CostEstimate(flops=3_000_000_000, bytes_accessed=8_000_000, transcendentals=0),
    )(core, act, sel, grad)


def per_device(
    activations,
    output_grad,
    weight_grad,
    input_basis,
    input_eigen,
    output_basis,
    output_eigen,
    input_factor,
    output_factor,
):
    xh, c = lax.axis_index("xh"), lax.axis_index("c")
    m = lax.axis_index(MP)
    tokens = activations.shape[0] * 32

    halves = jnp.stack([weight_grad[:, :384], weight_grad[:, 384:]])
    send = jnp.broadcast_to(halves[None], (8, 2, 96, 384)).reshape(16, 96, 384)
    grad_rows = lax.all_to_all(send, ("z", "c"), 0, 0).reshape(1536, 384)

    basis_out = output_basis[0]
    basis_far = lax.ppermute(basis_out, "xh", swap)
    basis_pair = jnp.where(xh == 0, jnp.stack([basis_out, basis_far]), jnp.stack([basis_far, basis_out]))
    basis_all = lax.all_gather(basis_pair, ("z", "c"), axis=0)
    v = basis_all.transpose(1, 0, 2, 3).reshape(768, 768)

    selected = lax.dynamic_slice_in_dim(activations, m * 192, 192, 1)
    sel = jnp.stack([jnp.pad(selected, ((0, 0), (0, 192))), jnp.pad(selected, ((0, 0), (192, 0)))])
    mine, other = factor_parts(c.astype(jnp.int32).reshape(1), activations, sel, output_grad)
    came = lax.ppermute(other, "c", swap)
    pair = (mine.astype(f32) + came.astype(f32)).astype(bf16)
    summed = lax.psum_scatter(pair, "z", scatter_dimension=0, tiled=False)
    in_sum = summed[:96].reshape(96, 2, 192)
    out_sum = summed[96:].reshape(2, 2, 24, 384)
    in_came = lax.ppermute(pick(in_sum, 1 - xh, 1), "xh", swap)
    out_came = lax.ppermute(pick(out_sum, 1 - xh, 1), "xh", swap)
    in_total = pick(in_sum, xh, 1).astype(f32) + in_came.astype(f32)
    out_total = pick(out_sum, xh, 1).astype(f32) + out_came.astype(f32)
    new_input = keep_rate * input_factor + (1.0 - keep_rate) * (in_total.T / tokens)
    new_output = keep_rate * output_factor + (1.0 - keep_rate) * (
        out_total.transpose(1, 0, 2).reshape(1, 24, 768) / tokens
    )

    ut = input_basis.T
    ut_mine = lax.dynamic_slice_in_dim(ut, xh * 1536, 1536, 1)
    ut_other = lax.dynamic_slice_in_dim(ut, (1 - xh) * 1536, 1536, 1)
    ut_far = lax.ppermute(ut_other, "xh", swap)
    near = jnp.where(xh == 0, jnp.stack([ut_mine, ut_far]), jnp.stack([ut_far, ut_mine]))
    far = lax.ppermute(near, "c", swap)
    block = jnp.where(c == 0, jnp.stack([near, far], axis=1), jnp.stack([far, near], axis=1)).reshape(384, 1536)

    grad_rows, pair_done = lax.optimization_barrier((grad_rows, pair))
    left_part = dot(block, grad_rows, 1, 0).astype(bf16).reshape(4, 96, 384)
    left_parts = lax.all_to_all(left_part, QUAD, 0, 0).astype(f32).reshape(2, 2, 96, 384)
    left_two = (left_parts[0] + left_parts[1]).astype(bf16)
    left = jnp.concatenate([left_two[0], left_two[1]], axis=1)
    rotated = dot(left, v, 1, 0)
    denominator = input_eigen[:, None] * output_eigen[0][None, :] + damping
    scaled = (rotated / denominator).astype(bf16)
    back = dot(scaled, v, 1, 1).astype(bf16)

    back_halves = jnp.stack([back[:, :384], back[:, 384:]])
    send = jnp.broadcast_to(back_halves[None], (2, 2, 96, 384)).reshape(4, 96, 384)
    back_group = lax.all_to_all(send, QUAD, 0, 0).reshape(384, 384)
    out_part = dot(block, back_group, 0, 0).astype(bf16).reshape(16, 96, 384)
    out_parts = lax.all_to_all(out_part, ("z", "c"), 0, 0).reshape(8, 2, 96, 384)
    total = jnp.sum(out_parts.astype(f32), axis=0).astype(bf16)
    result = jnp.concatenate([total[0], total[1]], axis=1)
    return (new_input, new_output, result)


def solution(mesh):
    fine = Mesh(mesh.devices.reshape(2, 8, 2, 2, 8), DP + MP)
    placed = (
        P(DP, None),
        P(DP, MP),
        P(DP, MP),
        P(None, DP),
        P(DP),
        P(MP, DP, None),
        P(MP, None),
        P(MP, DP),
        P(MP, DP, None),
    )
    return jax.shard_map(
        per_device,
        mesh=fine,
        in_specs=placed,
        out_specs=(P(MP, DP), P(MP, DP, None), P(DP, MP)),
        check_vma=False,
    )
```

```python
import jax
import jax.numpy as jnp
from jax import lax
from jax.experimental import pallas as pl
from jax.experimental.pallas import tpu as pltpu
from jax.sharding import Mesh, PartitionSpec as P

keep_rate = 0.95
damping = 0.03
swap = ((0, 1), (1, 0))
DP = ("xh", "z", "c")
MP = ("xl", "y")
bf16, f32 = jnp.bfloat16, jnp.float32


def dot(a, b, da, db):
    return lax.dot_general(a, b, (((da,), (db,)), ((), ())), preferred_element_type=f32)


def pick(a, index, axis):
    return lax.dynamic_index_in_dim(a, index, axis, keepdims=False)


def factor_kernel(core, act, sel, grad, mine, other, t_in, t_out):
    c = core[0]
    for j in range(4):
        low = act[:, j * 384 : (j + 1) * 384]
        high = act[:, 1536 + j * 384 : 1536 + (j + 1) * 384]
        t_in[j * 384 : (j + 1) * 384, :] = (dot(low, sel[0], 0, 0) + dot(high, sel[1], 0, 0)).astype(bf16)
    for j in range(2):
        t_out[j * 384 : (j + 1) * 384, :] = dot(grad[:, j * 384 : (j + 1) * 384], grad[...], 0, 0)
    for target, core_at in ((mine, c), (other, 1 - c)):
        for z in range(8):
            row = pl.multiple_of(z * 192 + core_at * 96, 96)
            target[z, 0:96, :] = t_in[pl.ds(row, 96), :]
            row = pl.multiple_of(z * 48 + core_at * 24, 24)
            first, second = t_out[pl.ds(row, 24), :], t_out[pl.ds(pl.multiple_of(384 + row, 24), 24), :]
            pair = jnp.concatenate([first, second], axis=0).astype(bf16)
            target[z, 96:144, :] = pair[:, :384]
            target[z, 144:192, :] = pair[:, 384:]


def factor_parts(core, act, sel, grad):
    vmem = pl.BlockSpec(memory_space=pltpu.VMEM)
    return pl.pallas_call(
        factor_kernel,
        out_shape=[jax.ShapeDtypeStruct((8, 192, 384), bf16)] * 2,
        in_specs=[pl.BlockSpec(memory_space=pltpu.SMEM), vmem, vmem, vmem],
        out_specs=[vmem, vmem],
        scratch_shapes=[pltpu.VMEM((1536, 384), bf16), pltpu.VMEM((768, 768), f32)],
        compiler_params=pltpu.CompilerParams(vmem_limit_bytes=32 * 1024 * 1024),
        cost_estimate=pl.CostEstimate(flops=3_000_000_000, bytes_accessed=8_000_000, transcendentals=0),
    )(core, act, sel, grad)


def per_device(
    activations,
    output_grad,
    weight_grad,
    input_basis,
    input_eigen,
    output_basis,
    output_eigen,
    input_factor,
    output_factor,
):
    xh, c = lax.axis_index("xh"), lax.axis_index("c")
    m = lax.axis_index(MP)
    tokens = activations.shape[0] * 32

    rows = jnp.concatenate([weight_grad, output_basis[0]], axis=0)
    halves = jnp.stack([rows[:, :384], rows[:, 384:]])
    send = jnp.broadcast_to(halves[None], (8, 2, 120, 384)).reshape(16, 120, 384)
    came_rows = lax.all_to_all(send, ("z", "c"), 0, 0)

    selected = lax.dynamic_slice_in_dim(activations, m * 192, 192, 1)
    sel = jnp.stack([jnp.pad(selected, ((0, 0), (0, 192))), jnp.pad(selected, ((0, 0), (192, 0)))])
    mine, other = factor_parts(c.astype(jnp.int32).reshape(1), activations, sel, output_grad)
    came = lax.ppermute(other, "c", swap)
    pair = (mine.astype(f32) + came.astype(f32)).astype(bf16)
    basis_in, _ = lax.optimization_barrier((input_basis, send))
    ut = basis_in.T
    ut_mine = lax.dynamic_slice_in_dim(ut, xh * 1536, 1536, 1)
    ut_other = lax.dynamic_slice_in_dim(ut, (1 - xh) * 1536, 1536, 1)
    ut_far = lax.ppermute(ut_other, "xh", swap)
    near = jnp.where(xh == 0, jnp.stack([ut_mine, ut_far]), jnp.stack([ut_far, ut_mine]))
    far = lax.ppermute(near, "c", swap)
    block = jnp.concatenate([near, far], axis=0).reshape(384, 1536)

    eigen_far = lax.ppermute(input_eigen, "xh", swap)
    came_rows, pair, eigen_far = lax.optimization_barrier((came_rows, pair, eigen_far))
    left_part = dot(block, came_rows[:, :96].reshape(1536, 384), 1, 0)
    left_send, v_mine, pair = lax.optimization_barrier((left_part.astype(bf16), came_rows[:, 96:].reshape(384, 384), pair))
    left_came = lax.ppermute(left_send, "xh", swap)
    v_came = lax.ppermute(v_mine, "xh", swap)
    v_near = jnp.where(xh == 0, jnp.concatenate([v_mine, v_came]), jnp.concatenate([v_came, v_mine]))
    v_far = lax.ppermute(v_near, "c", swap)
    v = jnp.concatenate([v_near, v_far], axis=1)
    left_half = (left_part + left_came.astype(f32)).astype(bf16)
    left_far = lax.ppermute(left_half[192:], "c", swap)
    left = jnp.where(
        c == 0,
        jnp.concatenate([left_half[:192], left_far], axis=1),
        jnp.concatenate([left_far, left_half[:192]], axis=1),
    )
    rotated = dot(left, v, 1, 0)
    eigen = jnp.where(xh == 0, jnp.stack([input_eigen, eigen_far]), jnp.stack([eigen_far, input_eigen]))
    eigen_out = output_eigen[0]
    eigen_out = jnp.where(c == 0, eigen_out, jnp.concatenate([eigen_out[384:], eigen_out[:384]]))
    denominator = eigen.reshape(192, 1) * eigen_out[None, :] + damping
    scaled = (rotated / denominator).astype(bf16)
    back = dot(scaled, v, 1, 1).astype(bf16)

    low, high = back[:, :384], back[:, 384:]
    back_far = lax.ppermute(jnp.where(c == 0, high, low), "c", swap)
    back_group = jnp.concatenate([jnp.where(c == 0, low, high), back_far], axis=0)
    out_part = dot(block, back_group, 0, 0).astype(bf16).reshape(16, 96, 384)
    came = lax.all_to_all(pair, "z", 0, 0)
    out_part, came = lax.optimization_barrier((out_part, came))
    summed = jnp.sum(came.astype(f32), axis=0).astype(bf16)
    in_sum = summed[:96].reshape(96, 2, 192)
    out_sum = summed[96:].reshape(2, 2, 24, 384)
    in_came = lax.ppermute(pick(in_sum, 1 - xh, 1), "xh", swap)
    out_came = lax.ppermute(pick(out_sum, 1 - xh, 1), "xh", swap)
    in_total = pick(in_sum, xh, 1).astype(f32) + in_came.astype(f32)
    out_total = pick(out_sum, xh, 1).astype(f32) + out_came.astype(f32)
    new_input = keep_rate * input_factor + (1.0 - keep_rate) * (in_total.T / tokens)
    new_output = keep_rate * output_factor + (1.0 - keep_rate) * (
        out_total.transpose(1, 0, 2).reshape(1, 24, 768) / tokens
    )

    out_parts = lax.all_to_all(out_part, ("z", "c"), 0, 0).reshape(8, 2, 96, 384)
    total = jnp.sum(out_parts.astype(f32), axis=0).astype(bf16)
    result = jnp.concatenate([total[0], total[1]], axis=1)
    return (new_input, new_output, result)


def solution(mesh):
    fine = Mesh(mesh.devices.reshape(2, 8, 2, 2, 8), DP + MP)
    placed = (
        P(DP, None),
        P(DP, MP),
        P(DP, MP),
        P(None, DP),
        P(DP),
        P(MP, DP, None),
        P(MP, None),
        P(MP, DP),
        P(MP, DP, None),
    )
    return jax.shard_map(
        per_device,
        mesh=fine,
        in_specs=placed,
        out_specs=(P(MP, DP), P(MP, DP, None), P(DP, MP)),
        check_vma=False,
    )
```

```python
import jax
import jax.numpy as jnp
from jax import lax
from jax.experimental import pallas as pl
from jax.experimental.pallas import tpu as pltpu
from jax.sharding import Mesh, PartitionSpec as P

keep_rate = 0.95
damping = 0.03
swap = ((0, 1), (1, 0))
DP = ("xh", "z", "c")
MP = ("xl", "y")
bf16, f32 = jnp.bfloat16, jnp.float32


def dot(a, b, da, db):
    return lax.dot_general(a, b, (((da,), (db,)), ((), ())), preferred_element_type=f32)


def pick(a, index, axis):
    return lax.dynamic_index_in_dim(a, index, axis, keepdims=False)


def factor_kernel(place, act, sel, grad, mine, other, t_in, t_out):
    xh, c = place[0], place[1]
    for j in range(8):
        t_in[j * 384 : (j + 1) * 384, :] = dot(act[:, j * 384 : (j + 1) * 384], sel[...], 0, 0)
    for j in range(2):
        t_out[j * 384 : (j + 1) * 384, :] = dot(grad[:, j * 384 : (j + 1) * 384], grad[...], 0, 0)
    for target, core_at in ((mine, c), (other, 1 - c)):
        for side, half in ((0, xh), (1, 1 - xh)):
            for z in range(8):
                row = pl.multiple_of(half * 1536 + z * 192 + core_at * 96, 96)
                low, high = t_in[pl.ds(row, 48), :], t_in[pl.ds(pl.multiple_of(row + 48, 48), 48), :]
                target[z, side, 0:48, :] = jnp.concatenate([low, high], axis=1).astype(bf16)
                row = pl.multiple_of(half * 384 + z * 48 + core_at * 24, 24)
                part = t_out[pl.ds(row, 24), :]
                target[z, side, 48:96, :] = jnp.concatenate([part[:, :384], part[:, 384:]], axis=0).astype(bf16)


def factor_parts(place, act, sel, grad):
    vmem = pl.BlockSpec(memory_space=pltpu.VMEM)
    return pl.pallas_call(
        factor_kernel,
        out_shape=[jax.ShapeDtypeStruct((8, 2, 96, 384), bf16)] * 2,
        in_specs=[pl.BlockSpec(memory_space=pltpu.SMEM), vmem, vmem, vmem],
        out_specs=[vmem, vmem],
        scratch_shapes=[pltpu.VMEM((3072, 192), f32), pltpu.VMEM((768, 768), f32)],
        compiler_params=pltpu.CompilerParams(vmem_limit_bytes=32 * 1024 * 1024),
        cost_estimate=pl.CostEstimate(flops=1_250_000_000, bytes_accessed=8_000_000, transcendentals=0),
    )(place, act, sel, grad)


def left_kernel(near, far, came, eigen, wide, narrow, v, rows):
    for s in range(16):
        rows[s * 96 : (s + 1) * 96, :] = came[s, :96, :]
    for at, basis in ((0, near), (192, far)):
        left = dot(basis[...], rows[...], 1, 0)
        wide[at : at + 192, :] = left
        narrow[at : at + 192, :] = left.astype(bf16)
    for s in range(8):
        v[s * 48 : (s + 1) * 48, :] = came[2 * s : 2 * s + 2, 96:, :].reshape(48, 384)
    rest, parts = eigen[...], []
    for _ in range(3):
        parts.append(rest.astype(bf16).astype(f32))
        rest = rest - parts[-1]
    three = jnp.concatenate(parts + [jnp.zeros((13, 128), f32)], axis=0).astype(bf16)
    v[384:, :] = jnp.concatenate([three, jnp.zeros((16, 256), bf16)], axis=1)


def left_parts(near, far, came, eigen):
    vmem = pl.BlockSpec(memory_space=pltpu.VMEM)
    return pl.pallas_call(
        left_kernel,
        out_shape=[
            jax.ShapeDtypeStruct((384, 384), f32),
            jax.ShapeDtypeStruct((384, 384), bf16),
            jax.ShapeDtypeStruct((400, 384), bf16),
        ],
        in_specs=[vmem] * 4,
        out_specs=[vmem] * 3,
        scratch_shapes=[pltpu.VMEM((1536, 384), bf16)],
        compiler_params=pltpu.CompilerParams(vmem_limit_bytes=16 * 1024 * 1024),
        cost_estimate=pl.CostEstimate(flops=453_000_000, bytes_accessed=3_600_000, transcendentals=0),
    )(near, far, came, eigen)


def column(row):
    ids = lax.broadcasted_iota(jnp.int32, (96, 128), 0) == lax.broadcasted_iota(jnp.int32, (96, 128), 1)
    return jnp.sum(jnp.where(ids, jnp.broadcast_to(row, (96, 128)), 0.0), axis=1, keepdims=True)


def middle_kernel(place, near, far, near_v, far_v, near_v_core, far_v_core, eigen, eigen_out, keep, send):
    same = place[0] == place[1]
    first = jnp.where(same, near[...], far[...])
    second = jnp.where(same, far[...], near[...])
    three = far_v[384:, :128].astype(f32)
    mine, other = column(eigen[...]), column(three[0:1] + three[1:2] + three[2:3])
    low, high = jnp.concatenate([mine, other], axis=0), jnp.concatenate([other, mine], axis=0)
    eigen_rows = jnp.where(place[0] == 0, low, high)
    scaled = []
    for at, (v_first, v_second) in enumerate(((near_v, far_v), (near_v_core, far_v_core))):
        rotated = dot(first, v_first[:384, :], 1, 0) + dot(second, v_second[:384, :], 1, 0)
        denominator = eigen_rows * eigen_out[:, at * 384 : (at + 1) * 384] + damping
        scaled.append((rotated / denominator).astype(bf16))
    back_first = dot(scaled[0], near_v[:384, :], 1, 1) + dot(scaled[1], near_v_core[:384, :], 1, 1)
    back_second = dot(scaled[0], far_v[:384, :], 1, 1) + dot(scaled[1], far_v_core[:384, :], 1, 1)
    keep[...] = jnp.where(same, back_first, back_second).astype(bf16)
    send[...] = jnp.where(same, back_second, back_first).astype(bf16)


def middle(place, *arrays):
    vmem = pl.BlockSpec(memory_space=pltpu.VMEM)
    return pl.pallas_call(
        middle_kernel,
        out_shape=[jax.ShapeDtypeStruct((192, 384), bf16)] * 2,
        in_specs=[pl.BlockSpec(memory_space=pltpu.SMEM)] + [vmem] * len(arrays),
        out_specs=[vmem, vmem],
        compiler_params=pltpu.CompilerParams(vmem_limit_bytes=16 * 1024 * 1024),
        cost_estimate=pl.CostEstimate(flops=453_000_000, bytes_accessed=2_000_000, transcendentals=0),
    )(place, *arrays)


def out_kernel(near, far, keep, came, out):
    for j in range(4):
        part = dot(near[:, j * 384 : (j + 1) * 384], keep[...], 0, 0)
        part += dot(far[:, j * 384 : (j + 1) * 384], came[...], 0, 0)
        for i in range(4):
            out[j * 4 + i] = part[i * 96 : (i + 1) * 96, :].astype(bf16)


def out_parts_of(near, far, keep, came):
    vmem = pl.BlockSpec(memory_space=pltpu.VMEM)
    return pl.pallas_call(
        out_kernel,
        out_shape=jax.ShapeDtypeStruct((16, 96, 384), bf16),
        in_specs=[vmem] * 4,
        out_specs=vmem,
        compiler_params=pltpu.CompilerParams(vmem_limit_bytes=16 * 1024 * 1024),
        cost_estimate=pl.CostEstimate(flops=453_000_000, bytes_accessed=2_800_000, transcendentals=0),
    )(near, far, keep, came)


def per_device(
    activations,
    output_grad,
    weight_grad,
    input_basis,
    input_eigen,
    output_basis,
    output_eigen,
    input_factor,
    output_factor,
):
    xh, c = lax.axis_index("xh"), lax.axis_index("c")
    m = lax.axis_index(MP)
    tokens = activations.shape[0] * 32

    rows = jnp.concatenate([weight_grad, output_basis[0]], axis=0)
    halves = jnp.stack([rows[:, :384], rows[:, 384:]])
    send = jnp.broadcast_to(halves[None], (8, 2, 120, 384)).reshape(16, 120, 384)
    came_rows = lax.all_to_all(send, ("z", "c"), 0, 0)

    basis_in, _ = lax.optimization_barrier((input_basis, send))
    ut = basis_in.T
    ut_mine = lax.dynamic_slice_in_dim(ut, xh * 1536, 1536, 1)
    ut_other = lax.dynamic_slice_in_dim(ut, (1 - xh) * 1536, 1536, 1)
    ut_far = lax.ppermute(ut_other, "xh", swap)

    activations, _ = lax.optimization_barrier((activations, send))
    selected = lax.dynamic_slice_in_dim(activations, m * 192, 192, 1)
    place = jnp.stack([xh, c]).astype(jnp.int32)
    mine, other = factor_parts(place, activations, selected, output_grad)
    other, ut_far = lax.optimization_barrier((other, ut_far))
    came = lax.ppermute(other, "c", swap)
    pair = (mine.astype(f32) + came.astype(f32)).astype(bf16)

    near = jnp.where(xh == 0, jnp.stack([ut_mine, ut_far]), jnp.stack([ut_far, ut_mine]))
    near = near.reshape(192, 1536)
    far = lax.ppermute(near, "c", swap)

    came_rows, pair, far = lax.optimization_barrier((came_rows, pair, far))
    eigen = jnp.pad(input_eigen, (0, 32)).reshape(1, 128)
    left_part, left_send, v_near = left_parts(near, far, came_rows, eigen)
    left_came = lax.ppermute(left_send, "xh", swap)
    v_far = lax.ppermute(v_near, "xh", swap)
    left_half = (left_part + left_came.astype(f32)).astype(bf16)
    left_far = lax.ppermute(left_half[192:], "c", swap)
    v_far, _ = lax.optimization_barrier((v_far, left_far))
    v_near_core, v_far_core = lax.ppermute(v_near, "c", swap), lax.ppermute(v_far, "c", swap)
    eigen_out = jnp.where(c == 0, output_eigen, jnp.concatenate([output_eigen[:, 384:], output_eigen[:, :384]], axis=1))
    keep, send_back = middle(
        place, left_half[:192], left_far, v_near, v_far, v_near_core, v_far_core, eigen, eigen_out
    )
    back_far = lax.ppermute(send_back, "c", swap)
    out_part = out_parts_of(near, far, keep, back_far)

    came = lax.all_to_all(pair, "z", 0, 0)
    out_part, came = lax.optimization_barrier((out_part, came))
    sides = jnp.sum(came.astype(f32), axis=0)
    total = sides[0] + lax.ppermute(sides[1].astype(bf16), "xh", swap).astype(f32)
    in_total = total[:48].reshape(48, 2, 192).transpose(2, 1, 0).reshape(192, 96)
    out_total = jnp.concatenate([total[48:72], total[72:]], axis=1)[None]
    new_input = keep_rate * input_factor + (1.0 - keep_rate) * (in_total / tokens)
    new_output = keep_rate * output_factor + (1.0 - keep_rate) * (out_total / tokens)

    out_parts = lax.all_to_all(out_part, ("z", "c"), 0, 0).reshape(8, 2, 96, 384)
    total = jnp.sum(out_parts.astype(f32), axis=0).astype(bf16)
    result = jnp.concatenate([total[0], total[1]], axis=1)
    return (new_input, new_output, result)


def solution(mesh):
    fine = Mesh(mesh.devices.reshape(2, 8, 2, 2, 8), DP + MP)
    placed = (
        P(DP, None),
        P(DP, MP),
        P(DP, MP),
        P(None, DP),
        P(DP),
        P(MP, DP, None),
        P(MP, None),
        P(MP, DP),
        P(MP, DP, None),
    )
    return jax.shard_map(
        per_device,
        mesh=fine,
        in_specs=placed,
        out_specs=(P(MP, DP), P(MP, DP, None), P(DP, MP)),
        check_vma=False,
    )
```

```python
import jax
import jax.numpy as jnp
from jax import lax
from jax.experimental import pallas as pl
from jax.experimental.pallas import tpu as pltpu
from jax.sharding import Mesh, PartitionSpec as P

keep_rate = 0.95
damping = 0.03
swap = ((0, 1), (1, 0))
DP = ("xh", "z", "c")
MP = ("xl", "y")
bf16, f32 = jnp.bfloat16, jnp.float32


def dot(a, b, da, db):
    return lax.dot_general(a, b, (((da,), (db,)), ((), ())), preferred_element_type=f32)


def pick(a, index, axis):
    return lax.dynamic_index_in_dim(a, index, axis, keepdims=False)


def factor_kernel(place, act, sel, grad, mine, other, t_in, t_out):
    xh, c = place[0], place[1]
    for j in range(8):
        t_in[j * 384 : (j + 1) * 384, :] = dot(act[:, j * 384 : (j + 1) * 384], sel[...], 0, 0)
    for j in range(2):
        t_out[j * 384 : (j + 1) * 384, :] = dot(grad[:, j * 384 : (j + 1) * 384], grad[...], 0, 0)
    for target, core_at in ((mine, c), (other, 1 - c)):
        for side, half in ((0, xh), (1, 1 - xh)):
            for z in range(8):
                row = pl.multiple_of(half * 1536 + z * 192 + core_at * 96, 96)
                low, high = t_in[pl.ds(row, 48), :], t_in[pl.ds(pl.multiple_of(row + 48, 48), 48), :]
                target[side, z, 0:48, :] = jnp.concatenate([low, high], axis=1).astype(bf16)
                row = pl.multiple_of(half * 384 + z * 48 + core_at * 24, 24)
                part = t_out[pl.ds(row, 24), :]
                target[side, z, 48:96, :] = jnp.concatenate([part[:, :384], part[:, 384:]], axis=0).astype(bf16)


def factor_parts(place, act, sel, grad):
    vmem = pl.BlockSpec(memory_space=pltpu.VMEM)
    return pl.pallas_call(
        factor_kernel,
        out_shape=[jax.ShapeDtypeStruct((2, 8, 96, 384), bf16)] * 2,
        in_specs=[pl.BlockSpec(memory_space=pltpu.SMEM), vmem, vmem, vmem],
        out_specs=[vmem, vmem],
        scratch_shapes=[pltpu.VMEM((3072, 192), f32), pltpu.VMEM((768, 768), f32)],
        compiler_params=pltpu.CompilerParams(vmem_limit_bytes=32 * 1024 * 1024),
        cost_estimate=pl.CostEstimate(flops=1_250_000_000, bytes_accessed=8_000_000, transcendentals=0),
    )(place, act, sel, grad)


def left_kernel(near, far, came, eigen, wide, narrow, v, rows):
    for s in range(16):
        rows[s * 96 : (s + 1) * 96, :] = came[s, :96, :]
    for at, basis in ((0, near), (192, far)):
        left = dot(basis[...], rows[...], 1, 0)
        wide[at : at + 192, :] = left
        narrow[at : at + 192, :] = left.astype(bf16)
    for s in range(8):
        v[s * 48 : (s + 1) * 48, :] = came[2 * s : 2 * s + 2, 96:, :].reshape(48, 384)
    rest, parts = eigen[...], []
    for _ in range(3):
        parts.append(rest.astype(bf16).astype(f32))
        rest = rest - parts[-1]
    three = jnp.concatenate(parts + [jnp.zeros((13, 128), f32)], axis=0).astype(bf16)
    v[384:, :] = jnp.concatenate([three, jnp.zeros((16, 256), bf16)], axis=1)


def left_parts(near, far, came, eigen):
    vmem = pl.BlockSpec(memory_space=pltpu.VMEM)
    return pl.pallas_call(
        left_kernel,
        out_shape=[
            jax.ShapeDtypeStruct((384, 384), f32),
            jax.ShapeDtypeStruct((384, 384), bf16),
            jax.ShapeDtypeStruct((400, 384), bf16),
        ],
        in_specs=[vmem] * 4,
        out_specs=[vmem] * 3,
        scratch_shapes=[pltpu.VMEM((1536, 384), bf16)],
        compiler_params=pltpu.CompilerParams(vmem_limit_bytes=16 * 1024 * 1024),
        cost_estimate=pl.CostEstimate(flops=453_000_000, bytes_accessed=3_600_000, transcendentals=0),
    )(near, far, came, eigen)


def column(row):
    ids = lax.broadcasted_iota(jnp.int32, (96, 128), 0) == lax.broadcasted_iota(jnp.int32, (96, 128), 1)
    return jnp.sum(jnp.where(ids, jnp.broadcast_to(row, (96, 128)), 0.0), axis=1, keepdims=True)


def tail_kernel(place, left, left_core, near_v, far_v, near_v_core, far_v_core, eigen, eigen_out, near, far, out):
    same = place[0] == place[1]

    def third(v):
        three = v[384:, :128].astype(f32)
        return column(three[0:1] + three[1:2] + three[2:3])

    half_first = jnp.where(same, near_v[:384, :], far_v[:384, :])
    half_second = jnp.where(same, near_v_core[:384, :], far_v_core[:384, :])
    backs = []
    for r, (mine, other) in enumerate(((column(eigen[...]), third(far_v)), (third(near_v_core), third(far_v_core)))):
        low, high = jnp.concatenate([mine, other], axis=0), jnp.concatenate([other, mine], axis=0)
        eigen_rows = jnp.where(place[0] == 0, low, high)
        own, came = left[r * 192 : (r + 1) * 192, :], left_core[(1 - r) * 192 : (2 - r) * 192, :]
        first, second = jnp.where(same, own, came), jnp.where(same, came, own)
        scaled = []
        for at, (v_first, v_second) in enumerate(((near_v, far_v), (near_v_core, far_v_core))):
            rotated = dot(first, v_first[:384, :], 1, 0) + dot(second, v_second[:384, :], 1, 0)
            denominator = eigen_rows * eigen_out[:, at * 384 : (at + 1) * 384] + damping
            scaled.append((rotated / denominator).astype(bf16))
        backs.append((dot(scaled[0], half_first, 1, 1) + dot(scaled[1], half_second, 1, 1)).astype(bf16))
    for j in range(4):
        part = dot(near[:, j * 384 : (j + 1) * 384], backs[0], 0, 0)
        part += dot(far[:, j * 384 : (j + 1) * 384], backs[1], 0, 0)
        for i in range(4):
            out[j * 4 + i] = part[i * 96 : (i + 1) * 96, :].astype(bf16)


def tail(place, *arrays):
    vmem = pl.BlockSpec(memory_space=pltpu.VMEM)
    return pl.pallas_call(
        tail_kernel,
        out_shape=jax.ShapeDtypeStruct((16, 96, 384), bf16),
        in_specs=[pl.BlockSpec(memory_space=pltpu.SMEM)] + [vmem] * len(arrays),
        out_specs=vmem,
        compiler_params=pltpu.CompilerParams(vmem_limit_bytes=24 * 1024 * 1024),
        cost_estimate=pl.CostEstimate(flops=1_130_000_000, bytes_accessed=4_800_000, transcendentals=0),
    )(place, *arrays)


def per_device(
    activations,
    output_grad,
    weight_grad,
    input_basis,
    input_eigen,
    output_basis,
    output_eigen,
    input_factor,
    output_factor,
):
    xh, c = lax.axis_index("xh"), lax.axis_index("c")
    m = lax.axis_index(MP)
    tokens = activations.shape[0] * 32

    rows = jnp.concatenate([weight_grad, output_basis[0]], axis=0)
    halves = jnp.stack([rows[:, :384], rows[:, 384:]])
    send = jnp.broadcast_to(halves[None], (8, 2, 120, 384)).reshape(16, 120, 384)
    came_rows = lax.all_to_all(send, ("z", "c"), 0, 0)

    basis_in, _ = lax.optimization_barrier((input_basis, send))
    ut = basis_in.T
    ut_mine = lax.dynamic_slice_in_dim(ut, xh * 1536, 1536, 1)
    ut_other = lax.dynamic_slice_in_dim(ut, (1 - xh) * 1536, 1536, 1)
    ut_far = lax.ppermute(ut_other, "xh", swap)

    selected = lax.dynamic_slice_in_dim(activations, m * 192, 192, 1)
    place = jnp.stack([xh, c]).astype(jnp.int32)
    mine, other = factor_parts(place, activations, selected, output_grad)
    other, ut_far = lax.optimization_barrier((other, ut_far))
    came = lax.ppermute(other, "c", swap)
    pair_far = (mine[1].astype(f32) + came[1].astype(f32)).astype(bf16)
    pair_near = (mine[0].astype(f32) + came[0].astype(f32)).astype(bf16)
    pair_near, _ = lax.optimization_barrier((pair_near, pair_far))
    came = lax.ppermute(pair_far, "xh", swap)
    four = (pair_near.astype(f32) + came.astype(f32)).astype(bf16)

    near = jnp.where(xh == 0, jnp.stack([ut_mine, ut_far]), jnp.stack([ut_far, ut_mine]))
    near = near.reshape(192, 1536)
    far = lax.ppermute(near, "c", swap)

    came_rows, pair_near, far = lax.optimization_barrier((came_rows, pair_near, far))
    eigen = jnp.pad(input_eigen, (0, 32)).reshape(1, 128)
    left_part, left_send, v_near = left_parts(near, far, came_rows, eigen)
    v_far = lax.ppermute(v_near, "xh", swap)
    v_near_core = lax.ppermute(v_near, "c", swap)
    left_came = lax.ppermute(left_send, "xh", swap)
    left_came, v_far = lax.optimization_barrier((left_came, v_far))
    left_half = (left_part + left_came.astype(f32)).astype(bf16)
    left_core = lax.ppermute(left_half, "c", swap)
    v_far_core = lax.ppermute(v_far, "c", swap)
    eigen_out = jnp.where(c == 0, output_eigen, jnp.concatenate([output_eigen[:, 384:], output_eigen[:, :384]], axis=1))
    out_part = tail(
        place, left_half, left_core, v_near, v_far, v_near_core, v_far_core, eigen, eigen_out, near, far
    )

    came = lax.all_to_all(four, "z", 0, 0)
    out_part, came = lax.optimization_barrier((out_part, came))
    total = jnp.sum(came.astype(f32), axis=0)
    in_total = total[:48].reshape(48, 2, 192).transpose(2, 1, 0).reshape(192, 96)
    out_total = jnp.concatenate([total[48:72], total[72:]], axis=1)[None]
    new_input = keep_rate * input_factor + (1.0 - keep_rate) * (in_total / tokens)
    new_output = keep_rate * output_factor + (1.0 - keep_rate) * (out_total / tokens)

    out_parts = lax.all_to_all(out_part, ("z", "c"), 0, 0).reshape(8, 2, 96, 384)
    total = jnp.sum(out_parts.astype(f32), axis=0).astype(bf16)
    result = jnp.concatenate([total[0], total[1]], axis=1)
    return (new_input, new_output, result)


def solution(mesh):
    fine = Mesh(mesh.devices.reshape(2, 8, 2, 2, 8), DP + MP)
    placed = (
        P(DP, None),
        P(DP, MP),
        P(DP, MP),
        P(None, DP),
        P(DP),
        P(MP, DP, None),
        P(MP, None),
        P(MP, DP),
        P(MP, DP, None),
    )
    return jax.shard_map(
        per_device,
        mesh=fine,
        in_specs=placed,
        out_specs=(P(MP, DP), P(MP, DP, None), P(DP, MP)),
        check_vma=False,
    )
```

```python
import jax
import jax.numpy as jnp
from jax import lax
from jax.experimental import pallas as pl
from jax.experimental.pallas import tpu as pltpu
from jax.sharding import Mesh, PartitionSpec as P

keep_rate = 0.95
damping = 0.03
swap = ((0, 1), (1, 0))
DP = ("xh", "z", "c")
MP = ("xl", "y")
bf16, f32 = jnp.bfloat16, jnp.float32


def dot(a, b, da, db):
    return lax.dot_general(a, b, (((da,), (db,)), ((), ())), preferred_element_type=f32)


def pick(a, index, axis):
    return lax.dynamic_index_in_dim(a, index, axis, keepdims=False)


def factor_kernel(place, act, sel, grad, mine, other, t_in, t_out):
    xh, c = place[0], place[1]
    for j in range(8):
        t_in[j * 384 : (j + 1) * 384, :] = dot(act[:, j * 384 : (j + 1) * 384], sel[...], 0, 0)
    for j in range(2):
        t_out[j * 384 : (j + 1) * 384, :] = dot(grad[:, j * 384 : (j + 1) * 384], grad[...], 0, 0)
    for target, core_at in ((mine, c), (other, 1 - c)):
        for side, half in ((0, xh), (1, 1 - xh)):
            for z in range(8):
                row = pl.multiple_of(half * 1536 + z * 192 + core_at * 96, 96)
                low, high = t_in[pl.ds(row, 48), :], t_in[pl.ds(pl.multiple_of(row + 48, 48), 48), :]
                target[side, z, 0:48, :] = jnp.concatenate([low, high], axis=1).astype(bf16)
                row = pl.multiple_of(half * 384 + z * 48 + core_at * 24, 24)
                part = t_out[pl.ds(row, 24), :]
                target[side, z, 48:96, :] = jnp.concatenate([part[:, :384], part[:, 384:]], axis=0).astype(bf16)


def factor_parts(place, act, sel, grad):
    vmem = pl.BlockSpec(memory_space=pltpu.VMEM)
    return pl.pallas_call(
        factor_kernel,
        out_shape=[jax.ShapeDtypeStruct((2, 8, 96, 384), bf16)] * 2,
        in_specs=[pl.BlockSpec(memory_space=pltpu.SMEM), vmem, vmem, vmem],
        out_specs=[vmem, vmem],
        scratch_shapes=[pltpu.VMEM((3072, 192), f32), pltpu.VMEM((768, 768), f32)],
        compiler_params=pltpu.CompilerParams(vmem_limit_bytes=32 * 1024 * 1024),
        cost_estimate=pl.CostEstimate(flops=1_250_000_000, bytes_accessed=8_000_000, transcendentals=0),
    )(place, act, sel, grad)


def left_kernel(near, far, came, eigen, out, rows):
    for s in range(16):
        rows[s * 96 : (s + 1) * 96, :] = came[s, :96, :]
    for at, basis in ((0, near), (192, far)):
        out[at : at + 192, :] = dot(basis[...], rows[...], 1, 0).astype(bf16)
    for s in range(8):
        out[384 + s * 48 : 384 + (s + 1) * 48, :] = came[2 * s : 2 * s + 2, 96:, :].reshape(48, 384)
    rest, parts = eigen[...], []
    for _ in range(3):
        parts.append(rest.astype(bf16).astype(f32))
        rest = rest - parts[-1]
    three = jnp.concatenate(parts + [jnp.zeros((13, 128), f32)], axis=0).astype(bf16)
    out[768:, :] = jnp.concatenate([three, jnp.zeros((16, 256), bf16)], axis=1)


def left_parts(near, far, came, eigen):
    vmem = pl.BlockSpec(memory_space=pltpu.VMEM)
    return pl.pallas_call(
        left_kernel,
        out_shape=jax.ShapeDtypeStruct((784, 384), bf16),
        in_specs=[vmem] * 4,
        out_specs=vmem,
        scratch_shapes=[pltpu.VMEM((1536, 384), bf16)],
        compiler_params=pltpu.CompilerParams(vmem_limit_bytes=16 * 1024 * 1024),
        cost_estimate=pl.CostEstimate(flops=453_000_000, bytes_accessed=3_600_000, transcendentals=0),
    )(near, far, came, eigen)


def column(row):
    ids = lax.broadcasted_iota(jnp.int32, (96, 128), 0) == lax.broadcasted_iota(jnp.int32, (96, 128), 1)
    return jnp.sum(jnp.where(ids, jnp.broadcast_to(row, (96, 128)), 0.0), axis=1, keepdims=True)


def tail_kernel(place, mine, mine_far, mine_core, far_core, eigen, eigen_out, near, far, out):
    same = place[0] == place[1]

    def third(group):
        three = group[768:, :128].astype(f32)
        return column(three[0:1] + three[1:2] + three[2:3])

    def left(one, two, at):
        return (one[at : at + 192, :].astype(f32) + two[at : at + 192, :].astype(f32)).astype(bf16)

    basis = slice(384, 768)
    half_first = jnp.where(same, mine[basis, :], mine_far[basis, :])
    half_second = jnp.where(same, mine_core[basis, :], far_core[basis, :])
    backs = []
    for r, (one, two) in enumerate(((column(eigen[...]), third(mine_far)), (third(mine_core), third(far_core)))):
        low, high = jnp.concatenate([one, two], axis=0), jnp.concatenate([two, one], axis=0)
        eigen_rows = jnp.where(place[0] == 0, low, high)
        own, came = left(mine, mine_far, r * 192), left(mine_core, far_core, (1 - r) * 192)
        first, second = jnp.where(same, own, came), jnp.where(same, came, own)
        scaled = []
        for at, (v_first, v_second) in enumerate(((mine, mine_far), (mine_core, far_core))):
            rotated = dot(first, v_first[basis, :], 1, 0) + dot(second, v_second[basis, :], 1, 0)
            denominator = eigen_rows * eigen_out[:, at * 384 : (at + 1) * 384] + damping
            scaled.append((rotated / denominator).astype(bf16))
        backs.append((dot(scaled[0], half_first, 1, 1) + dot(scaled[1], half_second, 1, 1)).astype(bf16))
    for j in range(4):
        part = dot(near[:, j * 384 : (j + 1) * 384], backs[0], 0, 0)
        part += dot(far[:, j * 384 : (j + 1) * 384], backs[1], 0, 0)
        for i in range(4):
            out[j * 4 + i] = part[i * 96 : (i + 1) * 96, :].astype(bf16)


def tail(place, *arrays):
    vmem = pl.BlockSpec(memory_space=pltpu.VMEM)
    return pl.pallas_call(
        tail_kernel,
        out_shape=jax.ShapeDtypeStruct((16, 96, 384), bf16),
        in_specs=[pl.BlockSpec(memory_space=pltpu.SMEM)] + [vmem] * len(arrays),
        out_specs=vmem,
        compiler_params=pltpu.CompilerParams(vmem_limit_bytes=24 * 1024 * 1024),
        cost_estimate=pl.CostEstimate(flops=1_130_000_000, bytes_accessed=4_800_000, transcendentals=0),
    )(place, *arrays)


def per_device(
    activations,
    output_grad,
    weight_grad,
    input_basis,
    input_eigen,
    output_basis,
    output_eigen,
    input_factor,
    output_factor,
):
    xh, c = lax.axis_index("xh"), lax.axis_index("c")
    m = lax.axis_index(MP)
    tokens = activations.shape[0] * 32

    rows = jnp.concatenate([weight_grad, output_basis[0]], axis=0)
    halves = jnp.stack([rows[:, :384], rows[:, 384:]])
    send = jnp.broadcast_to(halves[None], (8, 2, 120, 384)).reshape(16, 120, 384)
    came_rows = lax.all_to_all(send, ("z", "c"), 0, 0)

    basis_in, _ = lax.optimization_barrier((input_basis, send))
    ut = basis_in.T
    ut_mine = lax.dynamic_slice_in_dim(ut, xh * 1536, 1536, 1)
    ut_other = lax.dynamic_slice_in_dim(ut, (1 - xh) * 1536, 1536, 1)
    ut_far = lax.ppermute(ut_other, "xh", swap)

    selected = lax.dynamic_slice_in_dim(activations, m * 192, 192, 1)
    place = jnp.stack([xh, c]).astype(jnp.int32)
    mine, other = factor_parts(place, activations, selected, output_grad)
    other, ut_far = lax.optimization_barrier((other, ut_far))
    came = lax.ppermute(other, "c", swap)
    pair_far = (mine[1].astype(f32) + came[1].astype(f32)).astype(bf16)
    pair_near = (mine[0].astype(f32) + came[0].astype(f32)).astype(bf16)
    pair_near, _ = lax.optimization_barrier((pair_near, pair_far))
    came = lax.ppermute(pair_far, "xh", swap)
    four = (pair_near.astype(f32) + came.astype(f32)).astype(bf16)

    near = jnp.where(xh == 0, jnp.stack([ut_mine, ut_far]), jnp.stack([ut_far, ut_mine]))
    near = near.reshape(192, 1536)
    far = lax.ppermute(near, "c", swap)

    came_rows, pair_near, far = lax.optimization_barrier((came_rows, pair_near, far))
    eigen = jnp.pad(input_eigen, (0, 32)).reshape(1, 128)
    mine_rows = left_parts(near, far, came_rows, eigen)
    far_rows = lax.ppermute(mine_rows, "xh", swap)
    core_rows = lax.ppermute(mine_rows, "c", swap)
    far_core = lax.ppermute(far_rows, "c", swap)
    eigen_out = jnp.where(c == 0, output_eigen, jnp.concatenate([output_eigen[:, 384:], output_eigen[:, :384]], axis=1))
    out_part = tail(place, mine_rows, far_rows, core_rows, far_core, eigen, eigen_out, near, far)

    came = lax.all_to_all(four, "z", 0, 0)
    out_part, came = lax.optimization_barrier((out_part, came))
    total = jnp.sum(came.astype(f32), axis=0)
    in_total = total[:48].reshape(48, 2, 192).transpose(2, 1, 0).reshape(192, 96)
    out_total = jnp.concatenate([total[48:72], total[72:]], axis=1)[None]
    new_input = keep_rate * input_factor + (1.0 - keep_rate) * (in_total / tokens)
    new_output = keep_rate * output_factor + (1.0 - keep_rate) * (out_total / tokens)

    out_parts = lax.all_to_all(out_part, ("z", "c"), 0, 0).reshape(8, 2, 96, 384)
    total = jnp.sum(out_parts.astype(f32), axis=0).astype(bf16)
    result = jnp.concatenate([total[0], total[1]], axis=1)
    return (new_input, new_output, result)


def solution(mesh):
    fine = Mesh(mesh.devices.reshape(2, 8, 2, 2, 8), DP + MP)
    placed = (
        P(DP, None),
        P(DP, MP),
        P(DP, MP),
        P(None, DP),
        P(DP),
        P(MP, DP, None),
        P(MP, None),
        P(MP, DP),
        P(MP, DP, None),
    )
    return jax.shard_map(
        per_device,
        mesh=fine,
        in_specs=placed,
        out_specs=(P(MP, DP), P(MP, DP, None), P(DP, MP)),
        check_vma=False,
    )
```

```python
import jax
import jax.numpy as jnp
from jax import lax
from jax.experimental import pallas as pl
from jax.experimental.pallas import tpu as pltpu
from jax.sharding import Mesh, PartitionSpec as P

keep_rate = 0.95
damping = 0.03
swap = ((0, 1), (1, 0))
DP = ("xh", "z", "c")
MP = ("xl", "y")
bf16, f32 = jnp.bfloat16, jnp.float32


def dot(a, b, da, db):
    return lax.dot_general(a, b, (((da,), (db,)), ((), ())), preferred_element_type=f32)


def pick(a, index, axis):
    return lax.dynamic_index_in_dim(a, index, axis, keepdims=False)


def factor_kernel(place, act, sel, grad, mine, other, t_in, t_out):
    xh, c = place[0], place[1]
    for j in range(8):
        t_in[j * 384 : (j + 1) * 384, :] = dot(act[:, j * 384 : (j + 1) * 384], sel[...], 0, 0)
    for j in range(2):
        t_out[j * 384 : (j + 1) * 384, :] = dot(grad[:, j * 384 : (j + 1) * 384], grad[...], 0, 0)
    for target, core_at in ((mine, c), (other, 1 - c)):
        for side, half in ((0, xh), (1, 1 - xh)):
            for z in range(8):
                row = pl.multiple_of(half * 1536 + z * 192 + core_at * 96, 96)
                low, high = t_in[pl.ds(row, 48), :], t_in[pl.ds(pl.multiple_of(row + 48, 48), 48), :]
                target[side, z, 0:48, :] = jnp.concatenate([low, high], axis=1).astype(bf16)
                row = pl.multiple_of(half * 384 + z * 48 + core_at * 24, 24)
                part = t_out[pl.ds(row, 24), :]
                target[side, z, 48:96, :] = jnp.concatenate([part[:, :384], part[:, 384:]], axis=0).astype(bf16)


def factor_parts(place, act, sel, grad):
    vmem = pl.BlockSpec(memory_space=pltpu.VMEM)
    return pl.pallas_call(
        factor_kernel,
        out_shape=[jax.ShapeDtypeStruct((2, 8, 96, 384), bf16)] * 2,
        in_specs=[pl.BlockSpec(memory_space=pltpu.SMEM), vmem, vmem, vmem],
        out_specs=[vmem, vmem],
        scratch_shapes=[pltpu.VMEM((3072, 192), f32), pltpu.VMEM((768, 768), f32)],
        compiler_params=pltpu.CompilerParams(vmem_limit_bytes=32 * 1024 * 1024),
        cost_estimate=pl.CostEstimate(flops=1_250_000_000, bytes_accessed=8_000_000, transcendentals=0),
    )(place, act, sel, grad)


def left_kernel(near, far, came, eigen, out, rows):
    for s in range(16):
        rows[s * 96 : (s + 1) * 96, :] = came[s, :96, :]
    for at, basis in ((0, near), (192, far)):
        out[at : at + 192, :] = dot(basis[...], rows[...], 1, 0).astype(bf16)
    for s in range(8):
        out[384 + s * 48 : 384 + (s + 1) * 48, :] = came[2 * s : 2 * s + 2, 96:, :].reshape(48, 384)
    rest, parts = eigen[...], []
    for _ in range(3):
        parts.append(rest.astype(bf16).astype(f32))
        rest = rest - parts[-1]
    three = jnp.concatenate(parts + [jnp.zeros((13, 128), f32)], axis=0).astype(bf16)
    out[768:, :] = jnp.concatenate([three, jnp.zeros((16, 256), bf16)], axis=1)


def left_parts(near, far, came, eigen):
    vmem = pl.BlockSpec(memory_space=pltpu.VMEM)
    return pl.pallas_call(
        left_kernel,
        out_shape=jax.ShapeDtypeStruct((784, 384), bf16),
        in_specs=[vmem] * 4,
        out_specs=vmem,
        scratch_shapes=[pltpu.VMEM((1536, 384), bf16)],
        compiler_params=pltpu.CompilerParams(vmem_limit_bytes=16 * 1024 * 1024),
        cost_estimate=pl.CostEstimate(flops=453_000_000, bytes_accessed=3_600_000, transcendentals=0),
    )(near, far, came, eigen)


def column(row):
    ids = lax.broadcasted_iota(jnp.int32, (96, 128), 0) == lax.broadcasted_iota(jnp.int32, (96, 128), 1)
    return jnp.sum(jnp.where(ids, jnp.broadcast_to(row, (96, 128)), 0.0), axis=1, keepdims=True)


def tail_kernel(place, mine, mine_far, mine_core, far_core, eigen, eigen_out, near, far, out, held, sems):
    same = place[0] == place[1]

    def third(group):
        three = group[768:, :128].astype(f32)
        return column(three[0:1] + three[1:2] + three[2:3])

    def left(one, two, at):
        return (one[at : at + 192, :].astype(f32) + two[at : at + 192, :].astype(f32)).astype(bf16)

    basis = slice(384, 768)
    half_first = jnp.where(same, mine[basis, :], mine_far[basis, :])
    half_second = jnp.where(same, mine_core[basis, :], far_core[basis, :])
    backs = []
    for r, (one, two) in enumerate(((column(eigen[...]), third(mine_far)), (third(mine_core), third(far_core)))):
        low, high = jnp.concatenate([one, two], axis=0), jnp.concatenate([two, one], axis=0)
        eigen_rows = jnp.where(place[0] == 0, low, high)
        own, came = left(mine, mine_far, r * 192), left(mine_core, far_core, (1 - r) * 192)
        first, second = jnp.where(same, own, came), jnp.where(same, came, own)
        scaled = []
        for at, (v_first, v_second) in enumerate(((mine, mine_far), (mine_core, far_core))):
            rotated = dot(first, v_first[basis, :], 1, 0) + dot(second, v_second[basis, :], 1, 0)
            denominator = eigen_rows * eigen_out[:, at * 384 : (at + 1) * 384] + damping
            scaled.append((rotated / denominator).astype(bf16))
        backs.append((dot(scaled[0], half_first, 1, 1) + dot(scaled[1], half_second, 1, 1)).astype(bf16))
    copies = []
    for j in range(4):
        part = dot(near[:, j * 384 : (j + 1) * 384], backs[0], 0, 0)
        part += dot(far[:, j * 384 : (j + 1) * 384], backs[1], 0, 0)
        for i in range(4):
            held[j * 4 + i] = part[i * 96 : (i + 1) * 96, :].astype(bf16)
        quarter = pl.ds(j * 4, 4)
        copies.append(pltpu.make_async_copy(held.at[quarter], out.at[quarter], sems.at[j]))
        copies[-1].start()
    for copy in copies:
        copy.wait()


def tail(place, *arrays):
    vmem = pl.BlockSpec(memory_space=pltpu.VMEM)
    return pl.pallas_call(
        tail_kernel,
        out_shape=jax.ShapeDtypeStruct((16, 96, 384), bf16),
        in_specs=[pl.BlockSpec(memory_space=pltpu.SMEM)] + [vmem] * len(arrays),
        out_specs=pl.BlockSpec(memory_space=pltpu.HBM),
        scratch_shapes=[pltpu.VMEM((16, 96, 384), bf16), pltpu.SemaphoreType.DMA((4,))],
        compiler_params=pltpu.CompilerParams(vmem_limit_bytes=24 * 1024 * 1024),
        cost_estimate=pl.CostEstimate(flops=1_130_000_000, bytes_accessed=4_800_000, transcendentals=0),
    )(place, *arrays)


def per_device(
    activations,
    output_grad,
    weight_grad,
    input_basis,
    input_eigen,
    output_basis,
    output_eigen,
    input_factor,
    output_factor,
):
    xh, c = lax.axis_index("xh"), lax.axis_index("c")
    m = lax.axis_index(MP)
    tokens = activations.shape[0] * 32

    rows = jnp.concatenate([weight_grad, output_basis[0]], axis=0)
    halves = jnp.stack([rows[:, :384], rows[:, 384:]])
    send = jnp.broadcast_to(halves[None], (8, 2, 120, 384)).reshape(16, 120, 384)
    came_rows = lax.all_to_all(send, ("z", "c"), 0, 0)

    basis_in, _ = lax.optimization_barrier((input_basis, send))
    ut = basis_in.T
    ut_mine = lax.dynamic_slice_in_dim(ut, xh * 1536, 1536, 1)
    ut_other = lax.dynamic_slice_in_dim(ut, (1 - xh) * 1536, 1536, 1)
    ut_far = lax.ppermute(ut_other, "xh", swap)

    selected = lax.dynamic_slice_in_dim(activations, m * 192, 192, 1)
    place = jnp.stack([xh, c]).astype(jnp.int32)
    mine, other = factor_parts(place, activations, selected, output_grad)
    other, ut_far = lax.optimization_barrier((other, ut_far))
    came = lax.ppermute(other, "c", swap)
    pair_far = (mine[1].astype(f32) + came[1].astype(f32)).astype(bf16)
    pair_near = (mine[0].astype(f32) + came[0].astype(f32)).astype(bf16)
    pair_near, _ = lax.optimization_barrier((pair_near, pair_far))
    came = lax.ppermute(pair_far, "xh", swap)
    four = (pair_near.astype(f32) + came.astype(f32)).astype(bf16)

    near = jnp.where(xh == 0, jnp.stack([ut_mine, ut_far]), jnp.stack([ut_far, ut_mine]))
    near = near.reshape(192, 1536)
    far = lax.ppermute(near, "c", swap)

    came_rows, pair_near, far = lax.optimization_barrier((came_rows, pair_near, far))
    eigen = jnp.pad(input_eigen, (0, 32)).reshape(1, 128)
    mine_rows = left_parts(near, far, came_rows, eigen)
    far_rows = lax.ppermute(mine_rows, "xh", swap)
    core_rows = lax.ppermute(mine_rows, "c", swap)
    far_core = lax.ppermute(far_rows, "c", swap)
    eigen_out = jnp.where(c == 0, output_eigen, jnp.concatenate([output_eigen[:, 384:], output_eigen[:, :384]], axis=1))
    out_part = tail(place, mine_rows, far_rows, core_rows, far_core, eigen, eigen_out, near, far)

    came = lax.all_to_all(four, "z", 0, 0)
    out_part, came = lax.optimization_barrier((out_part, came))
    total = jnp.sum(came.astype(f32), axis=0)
    in_total = total[:48].reshape(48, 2, 192).transpose(2, 1, 0).reshape(192, 96)
    out_total = jnp.concatenate([total[48:72], total[72:]], axis=1)[None]
    new_input = keep_rate * input_factor + (1.0 - keep_rate) * (in_total / tokens)
    new_output = keep_rate * output_factor + (1.0 - keep_rate) * (out_total / tokens)

    out_parts = lax.all_to_all(out_part, ("z", "c"), 0, 0).reshape(8, 2, 96, 384)
    total = jnp.sum(out_parts.astype(f32), axis=0).astype(bf16)
    result = jnp.concatenate([total[0], total[1]], axis=1)
    return (new_input, new_output, result)


def solution(mesh):
    fine = Mesh(mesh.devices.reshape(2, 8, 2, 2, 8), DP + MP)
    placed = (
        P(DP, None),
        P(DP, MP),
        P(DP, MP),
        P(None, DP),
        P(DP),
        P(MP, DP, None),
        P(MP, None),
        P(MP, DP),
        P(MP, DP, None),
    )
    return jax.shard_map(
        per_device,
        mesh=fine,
        in_specs=placed,
        out_specs=(P(MP, DP), P(MP, DP, None), P(DP, MP)),
        check_vma=False,
    )
```

```python
import jax
import jax.numpy as jnp
from jax import lax
from jax.experimental import pallas as pl
from jax.experimental.pallas import tpu as pltpu
from jax.sharding import Mesh, PartitionSpec as P

keep_rate = 0.95
damping = 0.03
swap = ((0, 1), (1, 0))
DP = ("xh", "z", "c")
MP = ("xl", "y")
bf16, f32 = jnp.bfloat16, jnp.float32


def dot(a, b, da, db):
    return lax.dot_general(a, b, (((da,), (db,)), ((), ())), preferred_element_type=f32)


def pick(a, index, axis):
    return lax.dynamic_index_in_dim(a, index, axis, keepdims=False)


def factor_kernel(place, act, grad, mine, other, t_in, t_out):
    xh, c = place[0], place[1]
    both = act[:, pl.ds(pl.multiple_of(place[3] * 128, 128), 256)].astype(f32)
    sel = jnp.where(place[2] == 1, pltpu.roll(both, 192, 1), both)[:, :192].astype(bf16)
    for j in range(8):
        t_in[j * 384 : (j + 1) * 384, :] = dot(act[:, j * 384 : (j + 1) * 384], sel, 0, 0)
    for j in range(2):
        t_out[j * 384 : (j + 1) * 384, :] = dot(grad[:, j * 384 : (j + 1) * 384], grad[...], 0, 0)
    for target, core_at in ((mine, c), (other, 1 - c)):
        for side, half in ((0, xh), (1, 1 - xh)):
            for z in range(8):
                row = pl.multiple_of(half * 1536 + z * 192 + core_at * 96, 96)
                low, high = t_in[pl.ds(row, 48), :], t_in[pl.ds(pl.multiple_of(row + 48, 48), 48), :]
                target[side, z, 0:48, :] = jnp.concatenate([low, high], axis=1).astype(bf16)
                row = pl.multiple_of(half * 384 + z * 48 + core_at * 24, 24)
                part = t_out[pl.ds(row, 24), :]
                target[side, z, 48:96, :] = jnp.concatenate([part[:, :384], part[:, 384:]], axis=0).astype(bf16)


def factor_parts(place, act, grad):
    vmem = pl.BlockSpec(memory_space=pltpu.VMEM)
    return pl.pallas_call(
        factor_kernel,
        out_shape=[jax.ShapeDtypeStruct((2, 8, 96, 384), bf16)] * 2,
        in_specs=[pl.BlockSpec(memory_space=pltpu.SMEM), vmem, vmem],
        out_specs=[vmem, vmem],
        scratch_shapes=[pltpu.VMEM((3072, 192), f32), pltpu.VMEM((768, 768), f32)],
        compiler_params=pltpu.CompilerParams(vmem_limit_bytes=32 * 1024 * 1024),
        cost_estimate=pl.CostEstimate(flops=1_250_000_000, bytes_accessed=8_000_000, transcendentals=0),
    )(place, act, grad)


def left_kernel(near, far, came, eigen, out, rows):
    for s in range(16):
        rows[s * 96 : (s + 1) * 96, :] = came[s, :96, :]
    for at, basis in ((0, near), (192, far)):
        out[at : at + 192, :] = dot(basis[...], rows[...], 1, 0).astype(bf16)
    for s in range(8):
        out[384 + s * 48 : 384 + (s + 1) * 48, :] = came[2 * s : 2 * s + 2, 96:, :].reshape(48, 384)
    rest, parts = eigen[...], []
    for _ in range(3):
        parts.append(rest.astype(bf16).astype(f32))
        rest = rest - parts[-1]
    three = jnp.concatenate(parts + [jnp.zeros((13, 128), f32)], axis=0).astype(bf16)
    out[768:, :] = jnp.concatenate([three, jnp.zeros((16, 256), bf16)], axis=1)


def left_parts(near, far, came, eigen):
    vmem = pl.BlockSpec(memory_space=pltpu.VMEM)
    return pl.pallas_call(
        left_kernel,
        out_shape=jax.ShapeDtypeStruct((784, 384), bf16),
        in_specs=[vmem] * 4,
        out_specs=vmem,
        scratch_shapes=[pltpu.VMEM((1536, 384), bf16)],
        compiler_params=pltpu.CompilerParams(vmem_limit_bytes=16 * 1024 * 1024),
        cost_estimate=pl.CostEstimate(flops=453_000_000, bytes_accessed=3_600_000, transcendentals=0),
    )(near, far, came, eigen)


def column(row):
    ids = lax.broadcasted_iota(jnp.int32, (96, 128), 0) == lax.broadcasted_iota(jnp.int32, (96, 128), 1)
    return jnp.sum(jnp.where(ids, jnp.broadcast_to(row, (96, 128)), 0.0), axis=1, keepdims=True)


def tail_kernel(place, mine, mine_far, mine_core, far_core, eigen, eigen_out, near, far, out, held, sems):
    same = place[0] == place[1]

    def third(group):
        three = group[768:, :128].astype(f32)
        return column(three[0:1] + three[1:2] + three[2:3])

    def left(one, two, at):
        return (one[at : at + 192, :].astype(f32) + two[at : at + 192, :].astype(f32)).astype(bf16)

    basis = slice(384, 768)
    half_first = jnp.where(same, mine[basis, :], mine_far[basis, :])
    half_second = jnp.where(same, mine_core[basis, :], far_core[basis, :])
    backs = []
    for r, (one, two) in enumerate(((column(eigen[...]), third(mine_far)), (third(mine_core), third(far_core)))):
        low, high = jnp.concatenate([one, two], axis=0), jnp.concatenate([two, one], axis=0)
        eigen_rows = jnp.where(place[0] == 0, low, high)
        own, came = left(mine, mine_far, r * 192), left(mine_core, far_core, (1 - r) * 192)
        first, second = jnp.where(same, own, came), jnp.where(same, came, own)
        scaled = []
        for at, (v_first, v_second) in enumerate(((mine, mine_far), (mine_core, far_core))):
            rotated = dot(first, v_first[basis, :], 1, 0) + dot(second, v_second[basis, :], 1, 0)
            denominator = eigen_rows * eigen_out[:, at * 384 : (at + 1) * 384] + damping
            scaled.append((rotated / denominator).astype(bf16))
        backs.append((dot(scaled[0], half_first, 1, 1) + dot(scaled[1], half_second, 1, 1)).astype(bf16))
    copies = []
    for j in range(4):
        part = dot(near[:, j * 384 : (j + 1) * 384], backs[0], 0, 0)
        part += dot(far[:, j * 384 : (j + 1) * 384], backs[1], 0, 0)
        for i in range(4):
            held[j * 4 + i] = part[i * 96 : (i + 1) * 96, :].astype(bf16)
        quarter = pl.ds(j * 4, 4)
        copies.append(pltpu.make_async_copy(held.at[quarter], out.at[quarter], sems.at[j]))
        copies[-1].start()
    for copy in copies:
        copy.wait()


def tail(place, *arrays):
    vmem = pl.BlockSpec(memory_space=pltpu.VMEM)
    return pl.pallas_call(
        tail_kernel,
        out_shape=jax.ShapeDtypeStruct((16, 96, 384), bf16),
        in_specs=[pl.BlockSpec(memory_space=pltpu.SMEM)] + [vmem] * len(arrays),
        out_specs=pl.BlockSpec(memory_space=pltpu.HBM),
        scratch_shapes=[pltpu.VMEM((16, 96, 384), bf16), pltpu.SemaphoreType.DMA((4,))],
        compiler_params=pltpu.CompilerParams(vmem_limit_bytes=24 * 1024 * 1024),
        cost_estimate=pl.CostEstimate(flops=1_130_000_000, bytes_accessed=4_800_000, transcendentals=0),
    )(place, *arrays)


def per_device(
    activations,
    output_grad,
    weight_grad,
    input_basis,
    input_eigen,
    output_basis,
    output_eigen,
    input_factor,
    output_factor,
):
    xh, c = lax.axis_index("xh"), lax.axis_index("c")
    m = lax.axis_index(MP)
    tokens = activations.shape[0] * 32

    rows = jnp.concatenate([weight_grad, output_basis[0]], axis=0)
    halves = jnp.stack([rows[:, :384], rows[:, 384:]])
    send = jnp.broadcast_to(halves[None], (8, 2, 120, 384)).reshape(16, 120, 384)
    came_rows = lax.all_to_all(send, ("z", "c"), 0, 0)

    basis_in, _ = lax.optimization_barrier((input_basis, send))
    ut = basis_in.T
    ut_mine = lax.dynamic_slice_in_dim(ut, xh * 1536, 1536, 1)
    ut_other = lax.dynamic_slice_in_dim(ut, (1 - xh) * 1536, 1536, 1)
    ut_far = lax.ppermute(ut_other, "xh", swap)

    place = jnp.stack([xh, c, m % 2, (m * 3) // 2]).astype(jnp.int32)
    mine, other = factor_parts(place, activations, output_grad)
    other, ut_far = lax.optimization_barrier((other, ut_far))
    came = lax.ppermute(other, "c", swap)
    pair_far = (mine[1].astype(f32) + came[1].astype(f32)).astype(bf16)
    own, _ = lax.optimization_barrier((mine[0], pair_far))
    pair_near = (own.astype(f32) + came[0].astype(f32)).astype(bf16)
    sides_far = lax.ppermute(pair_far, "xh", swap)

    near = jnp.where(xh == 0, jnp.stack([ut_mine, ut_far]), jnp.stack([ut_far, ut_mine]))
    near = near.reshape(192, 1536)
    far = lax.ppermute(near, "c", swap)

    came_rows, pair_near, far = lax.optimization_barrier((came_rows, pair_near, far))
    eigen = jnp.pad(input_eigen, (0, 32)).reshape(1, 128)
    mine_rows = left_parts(near, far, came_rows, eigen)
    far_rows = lax.ppermute(mine_rows, "xh", swap)
    pair_near, _ = lax.optimization_barrier((pair_near, mine_rows))
    four = (pair_near.astype(f32) + sides_far.astype(f32)).astype(bf16)
    core_rows = lax.ppermute(mine_rows, "c", swap)
    far_core = lax.ppermute(far_rows, "c", swap)
    eigen_out = jnp.where(c == 0, output_eigen, jnp.concatenate([output_eigen[:, 384:], output_eigen[:, :384]], axis=1))
    out_part = tail(place, mine_rows, far_rows, core_rows, far_core, eigen, eigen_out, near, far)

    came = lax.all_to_all(four, "z", 0, 0)
    out_part, came = lax.optimization_barrier((out_part, came))
    total = jnp.sum(came.astype(f32), axis=0)
    in_total = total[:48].reshape(48, 2, 192).transpose(2, 1, 0).reshape(192, 96)
    out_total = jnp.concatenate([total[48:72], total[72:]], axis=1)[None]
    new_input = keep_rate * input_factor + (1.0 - keep_rate) * (in_total / tokens)
    new_output = keep_rate * output_factor + (1.0 - keep_rate) * (out_total / tokens)

    out_parts = lax.all_to_all(out_part, ("z", "c"), 0, 0).reshape(8, 2, 96, 384)
    total = jnp.sum(out_parts.astype(f32), axis=0).astype(bf16)
    result = jnp.concatenate([total[0], total[1]], axis=1)
    return (new_input, new_output, result)


def solution(mesh):
    fine = Mesh(mesh.devices.reshape(2, 8, 2, 2, 8), DP + MP)
    placed = (
        P(DP, None),
        P(DP, MP),
        P(DP, MP),
        P(None, DP),
        P(DP),
        P(MP, DP, None),
        P(MP, None),
        P(MP, DP),
        P(MP, DP, None),
    )
    return jax.shard_map(
        per_device,
        mesh=fine,
        in_specs=placed,
        out_specs=(P(MP, DP), P(MP, DP, None), P(DP, MP)),
        check_vma=False,
    )
```
